256 devices in a mesh: row: 16 (over z_hi, y, core), col: 16 (over x, z_lo).
Axes of the slice: x: 4, y: 4, z: 8 (z_hi: 2, z_lo: 4; z = z_hi * 4 + z_lo), core: 2. Of those that a mesh axis runs over, the one named last changes fastest.
Arguments:
- output_grad: bfloat16 [1024, 8192], P('col', 'row'), may hold values from -16 to 16
- gate_preact: bfloat16 [1024, 28672], P('row', 'col'), may hold values from -6 to 6
- up_preact: bfloat16 [1024, 28672], P('row', 'col'), may hold values from -6 to 6
- gate_weight: bfloat16 [8192, 28672], P('row', 'col'), may hold values from -0.0625 to 0.0625
- up_weight: bfloat16 [8192, 28672], P('row', 'col'), may hold values from -0.0625 to 0.0625
- down_weight: bfloat16 [28672, 8192], P('col', 'row'), may hold values from -0.03125 to 0.03125
Outputs:
- input_grad: bfloat16 [1024, 8192], P('col', 'row')
- gate_factor: float32 [14336, 28672], P('row', 'col')
The draws below stay inside these ranges and needn't reach their ends.
All inputs are finite; a program needn't handle non-finite values.
Results may differ from the reference program's by a relative error of at most 0.0049.
Values may be sent and summed in bfloat16 or wider, within the bound.
No kernel may reach another device: no remote copies, remote signals or barrier semaphores. Data moves between devices by JAX's collectives and lax.ppermute only.
A program may use at most 128 MiB of HBM per device.

```python
import jax
import jax.numpy as jnp

D = 8192
FF = 28672
TOKENS = 1024
SLAB = 14336


def block_scale(own_key, extent, pieces, low, high):
    level = 1.0
    for axis_at, shards_of in pieces:
        heights = jax.random.uniform(jax.random.fold_in(jax.random.fold_in(own_key, 6), axis_at), (shards_of,), jnp.float32, low / len(pieces), high / len(pieces))
        level = level * jnp.repeat(jnp.exp(heights), extent[axis_at] // shards_of).reshape((-1,) + (1,) * (len(extent) - 1 - axis_at))
    return level


def noise(key, dims, width, most, split=(), dtype=jnp.bfloat16):
    drawn = width * jax.random.normal(key, dims, jnp.float32)
    if split:
        drawn = drawn * block_scale(key, dims, split, -0.22, 0.18)
    return jnp.clip(drawn, -most, most).astype(dtype)


def setup_inputs(seed: int = 0) -> dict:
    key_list = jax.random.split(jax.random.key(seed), 7)
    return {
        "output_grad": noise(key_list[0], (TOKENS, D), 4.0, 16.0, ((0, 16), (1, 16))),
        "gate_preact": noise(key_list[1], (TOKENS, FF), 1.0, 6.0, ((0, 16), (1, 16))),
        "up_preact": noise(key_list[2], (TOKENS, FF), 1.0, 6.0, ((0, 16), (1, 16))),
        "gate_weight": noise(key_list[3], (D, FF), D ** -0.5, 0.0625, ((0, 16), (1, 16))),
        "up_weight": noise(key_list[4], (D, FF), D ** -0.5, 0.0625, ((0, 16), (1, 16))),
        "down_weight": noise(key_list[5], (FF, D), FF ** -0.5, 0.03125, ((0, 16), (1, 16))),
    }


def swiglu_grads(hidden_grad, gate_preact, up_preact):
    gate_float = gate_preact.astype(jnp.float32)
    up_float = up_preact.astype(jnp.float32)
    logistic = jax.nn.sigmoid(gate_float)
    derivative = logistic * (1.0 + gate_float * (1.0 - logistic))
    grad_gate = (hidden_grad * up_float * derivative).astype(jnp.bfloat16)
    grad_up = (hidden_grad * gate_float * logistic).astype(jnp.bfloat16)
    return grad_gate, grad_up


def reference(output_grad, gate_preact, up_preact, gate_weight, up_weight, down_weight):
    hidden_grad = jnp.dot(output_grad, down_weight.T, preferred_element_type=jnp.float32)
    grad_gate, grad_up = swiglu_grads(hidden_grad, gate_preact, up_preact)
    input_float = jnp.dot(grad_gate, gate_weight.T, preferred_element_type=jnp.float32)
    input_float = input_float + jnp.dot(grad_up, up_weight.T, preferred_element_type=jnp.float32)
    input_grad = input_float.astype(jnp.bfloat16)
    slab_grads = grad_gate[:, 0:SLAB]
    gate_factor = jnp.dot(slab_grads.T, grad_gate, preferred_element_type=jnp.float32) / TOKENS
    return input_grad, gate_factor
```

```python
import jax
import jax.numpy as jnp
from jax import lax
from jax.sharding import Mesh
from jax.sharding import PartitionSpec as P

TOKENS = 1024
BF = jnp.bfloat16
F32 = jnp.float32
SIZES = (2, 4, 2, 4, 4)
AXES = ("zh", "y", "core", "x", "zl")
ROW = ("zh", "y", "core")
COL = ("x", "zl")


def swap(block, axis, k):
    n = SIZES[AXES.index(axis)]
    return lax.ppermute(block, axis, [(i, i ^ k) for i in range(n)])


def put(buf, block, *index):
    start = list(index) + [0] * (buf.ndim - len(index))
    lead = buf.ndim - block.ndim
    return lax.dynamic_update_slice(buf, block.reshape((1,) * lead + block.shape), start)


def pick(array, index, axis):
    return lax.dynamic_index_in_dim(array, index, axis, keepdims=False)


def swiglu_grads(hidden_grad, gate_preact, up_preact):
    gate_float = gate_preact.astype(F32)
    up_float = up_preact.astype(F32)
    logistic = jax.nn.sigmoid(gate_float)
    derivative = logistic * (1.0 + gate_float * (1.0 - logistic))
    grad_gate = (hidden_grad * up_float * derivative).astype(BF)
    grad_up = (hidden_grad * gate_float * logistic).astype(BF)
    return (grad_gate, grad_up)


def contract_last(left, right):
    return lax.dot_general(
        left, right, (((left.ndim - 1,), (1,)), ((), ())), preferred_element_type=F32
    )


def scatter_pairs(half):
    pairs = []
    for zh in range(2):
        for y in range(4):
            for core in range(2):
                for x in range(2):
                    for zl in range(4):
                        src = (((zh * 4 + y) * 2 + core) * 4 + x) * 4 + zl
                        dst = (((x * 4 + zl) * 2 + half) * 4 + y) * 4 + core * 2 + zh
                        pairs.append((src, dst))
    return pairs


def shards(output_grad, gate_preact, up_preact, gate_weight, up_weight, down_weight):
    zh, y, core, x, zl = (lax.axis_index(a) for a in AXES)
    units = gate_preact.shape[1]
    half_units = units // 2
    width = output_grad.shape[1]

    def at_zl(buf, block, which):
        return put(buf, block, (which & 1) ^ core, which >> 1)

    run = jnp.zeros((2, 2, 64, width), BF)
    run = at_zl(run, output_grad, zl)
    for k in (1, 2, 3):
        run = at_zl(run, swap(output_grad, "zl", k), zl ^ k)
    cot = jnp.zeros((2, 4, 2, 64, width), BF)
    cot = lax.dynamic_update_slice(cot, run[:, None], (0, x, 0, 0, 0))
    for k in (1, 3, 2):
        cot = lax.dynamic_update_slice(cot, swap(run, "x", k)[:, None], (0, x ^ k, 0, 0, 0))
    pre = jnp.stack([gate_preact, up_preact])
    pre_far = swap(pre, "zh", 1)

    sent = contract_last(cot[1].reshape(512, width), down_weight).astype(BF)
    kept = contract_last(cot[0].reshape(512, width), down_weight)
    part = (kept + swap(sent, "core", 1).astype(F32)).reshape(2, 4, 64, units)
    hidden = pick(part, y, 1)
    got = [swap(pick(part, y ^ k, 1).astype(BF), "y", k) for k in (1, 3, 2)]
    for block in got:
        hidden = hidden + block.astype(F32)
    hidden = hidden + swap(hidden.astype(BF), "zh", 1).astype(F32)

    low = jnp.where(zh == 0, pre, pre_far)
    high = jnp.where(zh == 0, pre_far, pre)
    grad_gate, grad_up = swiglu_grads(
        hidden, jnp.stack([low[0], high[0]]), jnp.stack([low[1], high[1]])
    )

    own = pick(grad_gate, zh, 0)
    piece0 = lax.ppermute(own[:, :half_units], AXES, scatter_pairs(0))
    piece1 = lax.ppermute(own[:, half_units:], AXES, scatter_pairs(1))
    piece = jnp.where(core == 0, piece0, piece1)
    srun = put(jnp.zeros((4, 64, half_units), BF), piece, zl)
    for k in (1, 2, 3):
        srun = put(srun, swap(piece, "zl", k), zl ^ k)
    slab = put(jnp.zeros((4, 4, 64, half_units), BF), srun, x)

    both = jnp.stack([grad_gate, grad_up])
    run2 = jnp.zeros((2, 4, 2, 64, units), BF)
    run2 = lax.dynamic_update_slice(run2, both[:, None], (0, y, 0, 0, 0))
    for k in (1, 3, 2):
        run2 = lax.dynamic_update_slice(run2, swap(both, "y", k)[:, None], (0, y ^ k, 0, 0, 0))
    full = jnp.zeros((2, 4, 2, 2, 64, units), BF)
    full = lax.dynamic_update_slice(full, run2[:, :, None], (0, 0, core, 0, 0, 0))
    full = lax.dynamic_update_slice(
        full, swap(run2, "core", 1)[:, :, None], (0, 0, 1 - core, 0, 0, 0)
    )
    for k in (1, 3, 2):
        slab = put(slab, swap(srun, "x", k), x ^ k)

    gate_all = full[0].reshape(TOKENS, units)
    up_all = full[1].reshape(TOKENS, units)
    partial = contract_last(gate_all, gate_weight) + contract_last(up_all, up_weight)
    partial = partial.reshape(2, 2, 2, 2, 64, width).transpose(3, 0, 1, 2, 4, 5)
    partial = partial.reshape(4, 4, 64, width)
    mine = pick(partial, x, 0)
    for block in [swap(pick(partial, x ^ k, 0).astype(BF), "x", k) for k in (1, 3, 2)]:
        mine = mine + block.astype(F32)
    result = pick(mine, zl, 0)
    for block in [swap(pick(mine, zl ^ k, 0).astype(BF), "zl", k) for k in (1, 2, 3)]:
        result = result + block.astype(F32)

    gate_factor = (
        lax.dot_general(
            slab.reshape(TOKENS, half_units),
            gate_all,
            (((0,), (0,)), ((), ())),
            preferred_element_type=F32,
        )
        / TOKENS
    )
    return (result.astype(BF), gate_factor)


def solution(mesh):
    fine = Mesh(mesh.devices.reshape(SIZES), AXES)
    return jax.shard_map(
        shards,
        mesh=fine,
        in_specs=(P(COL, ROW), P(ROW, COL), P(ROW, COL), P(ROW, COL), P(ROW, COL), P(COL, ROW)),
        out_specs=(P(COL, ROW), P(ROW, COL)),
        check_vma=False,
    )
```

```python
import jax
import jax.numpy as jnp
from jax import lax
from jax.sharding import Mesh
from jax.sharding import PartitionSpec as P

TOKENS = 1024
ROWS = 32
BF = jnp.bfloat16
F32 = jnp.float32
SIZES = (2, 4, 2, 4, 4)
AXES = ("zh", "y", "core", "x", "zl")
ROW = ("zh", "y", "core")
COL = ("x", "zl")


def swap(block, axis, k):
    n = SIZES[AXES.index(axis)]
    return lax.ppermute(block, axis, [(i, i ^ k) for i in range(n)])


def after(block, *deps):
    return lax.optimization_barrier((block, deps))[0]


def put(buf, block, index, axis):
    start = [0] * buf.ndim
    start[axis] = index
    return lax.dynamic_update_slice(buf, jnp.expand_dims(block, axis), start)


def pick(array, index, axis):
    return lax.dynamic_index_in_dim(array, index, axis, keepdims=False)


def swiglu_grads(hidden_grad, gate_preact, up_preact):
    gate_float = gate_preact.astype(F32)
    up_float = up_preact.astype(F32)
    logistic = jax.nn.sigmoid(gate_float)
    derivative = logistic * (1.0 + gate_float * (1.0 - logistic))
    grad_gate = (hidden_grad * up_float * derivative).astype(BF)
    grad_up = (hidden_grad * gate_float * logistic).astype(BF)
    return (grad_gate, grad_up)


def contract_last(left, right):
    return lax.dot_general(left, right, (((1,), (1,)), ((), ())), preferred_element_type=F32)


def device(zh, y, core, x, zl):
    return (((zh * 4 + y) * 2 + core) * 4 + x) * 4 + zl


def scatter_pairs(half):
    pairs = []
    for zh in range(2):
        for y in range(4):
            for core in range(2):
                for x in range(2):
                    for zl in range(4):
                        dst = device(
                            x, zl, half, (core ^ half) * 2 + (y >> 1), (y & 1) * 2 + zh
                        )
                        pairs.append((device(zh, y, core, x, zl), dst))
    return pairs


def home_pairs(k):
    return [
        (core * 4 + zl, core * 4 + (zl ^ k))
        for core in range(2)
        for zl in range(4)
        if ((zl ^ k) & 1) == core
    ]


def shards(output_grad, gate_preact, up_preact, gate_weight, up_weight, down_weight):
    zh, y, core, x, zl = (lax.axis_index(a) for a in AXES)
    units = gate_preact.shape[1]
    half_units = units // 2
    width = output_grad.shape[1]

    def at_zl(buf, block, which):
        start = ((which & 1) ^ core, which >> 1, 0, 0)
        return lax.dynamic_update_slice(buf, block[None, None], start)

    down_far = swap(down_weight, "core", 1)
    run = at_zl(jnp.zeros((2, 2, 64, width), BF), output_grad, zl)
    for k in (1, 2, 3):
        run = at_zl(run, swap(output_grad, "zl", k), zl ^ k)
    pre = after(jnp.stack([gate_preact, up_preact]), run)
    pre_far = swap(pre, "zh", 1)
    cot = put(jnp.zeros((2, 4, 2, 64, width), BF), run, x, 1)
    for k in (1, 3, 2):
        cot = put(cot, swap(run, "x", k), x ^ k, 1)
    near = cot[0]
    far = swap(cot[1], "core", 1)
    gate_far = swap(after(gate_weight, cot), "core", 1)
    up_far = swap(after(up_weight, cot), "core", 1)

    low = jnp.where(zh == 0, pre, pre_far)
    high = jnp.where(zh == 0, pre_far, pre)
    gate_tok = jnp.stack([low[0], high[0]])
    up_tok = jnp.stack([low[1], high[1]])

    def part_of(c):
        rows = slice(c * ROWS, (c + 1) * ROWS)
        part = contract_last(near[:, :, rows].reshape(8 * ROWS, width), down_weight)
        part = part + contract_last(far[:, :, rows].reshape(8 * ROWS, width), down_far)
        return part.reshape(2, 4, ROWS, units)

    def over_y(part, *deps):
        sends = tuple(pick(part, y ^ k, 1).astype(BF) for k in (1, 3, 2))
        sends = after(sends, *deps)
        return [swap(s, "y", k) for s, k in zip(sends, (1, 3, 2))]

    def add_up(part, got):
        hidden = pick(part, y, 1)
        for block in got:
            hidden = hidden + block.astype(F32)
        return hidden

    def grads(c, hidden, far_hidden):
        rows = slice(c * ROWS, (c + 1) * ROWS)
        hidden = hidden + far_hidden.astype(F32)
        return swiglu_grads(hidden, gate_tok[:, rows], up_tok[:, rows])

    part_a = part_of(0)
    part_b = part_of(1)
    got_a = over_y(part_a)
    hidden_a = add_up(part_a, got_a)
    got_b = over_y(part_b, *got_a)
    hfar_a = swap(hidden_a.astype(BF), "zh", 1)
    gate_a, up_a = grads(0, hidden_a, hfar_a)
    both_a = jnp.stack([gate_a, up_a])
    hidden_b = add_up(part_b, got_b)
    hfar_b = swap(hidden_b.astype(BF), "zh", 1)
    both_a = after(both_a, *got_b)
    one_a = swap(both_a, "y", 1)
    three_a = swap(both_a, "y", 3)
    hfar_b, one_a, three_a = lax.optimization_barrier((hfar_b, one_a, three_a))
    gate_b, up_b = grads(1, hidden_b, hfar_b)
    both_b = jnp.stack([gate_b, up_b])

    own = jnp.concatenate([pick(gate_a, zh, 0), pick(gate_b, zh, 0)], 0)
    piece0 = lax.ppermute(own[:, :half_units], AXES, scatter_pairs(0))
    piece1 = lax.ppermute(own[:, half_units:], AXES, scatter_pairs(1))

    def forward(one, three):
        return swap(one[:, 0], "y", 3), swap(three[:, 1], "y", 1)

    def assemble(both, one, three, two):
        full = jnp.zeros((2, 4, 2, ROWS, units), BF)
        full = put(full, both, y, 1)
        full = put(full, one, y ^ 1, 1)
        full = put(full, three, y ^ 3, 1)
        return put(full, jnp.stack(two, 1), y ^ 2, 1)

    def project(full):
        gate_mine = full[0].reshape(8 * ROWS, units)
        up_mine = full[1].reshape(8 * ROWS, units)
        near_sum = contract_last(gate_mine, gate_weight) + contract_last(up_mine, up_weight)
        far_sum = contract_last(gate_mine, gate_far) + contract_last(up_mine, up_far)
        sums = jnp.stack([near_sum, far_sum]).reshape(2, 2, 2, 2, ROWS, width)
        return sums.transpose(3, 1, 2, 0, 4, 5).reshape(4, 2, 2, ROWS, width)

    two_a = forward(one_a, three_a)
    both_b, piece0, piece1, *two_a = lax.optimization_barrier((both_b, piece0, piece1, *two_a))
    piece = jnp.where(core == 0, piece0, piece1)
    one_b = swap(both_b, "y", 1)
    three_b = swap(both_b, "y", 3)
    got = [swap(piece, "zl", k) for k in (1, 2, 3)]
    one_b, three_b, *got = lax.optimization_barrier((one_b, three_b, *got))
    srun = put(jnp.zeros((4, 64, half_units), BF), piece, zl, 0)
    for k in (1, 2, 3):
        srun = put(srun, got[k - 1], zl ^ k, 0)
    two_b = forward(one_b, three_b)
    got = [swap(srun, "x", k) for k in (1, 3, 2)]
    full_a = assemble(both_a, one_a, three_a, two_a)
    full_b = assemble(both_b, one_b, three_b, two_b)
    partial = jnp.concatenate([project(full_a), project(full_b)], 3)
    gate_near = jnp.concatenate([full_a[0], full_b[0]], 2)
    gate_other = swap(gate_near, "core", 1)
    slab = put(jnp.zeros((4, 4, 64, half_units), BF), srun, x, 0)
    for block, k in zip(got, (1, 3, 2)):
        slab = put(slab, block, x ^ k, 0)
    gate_all = jnp.stack([gate_near, gate_other])
    gate_factor = (
        lax.dot_general(
            slab.reshape(TOKENS, half_units),
            gate_all.reshape(TOKENS, units),
            (((0,), (0,)), ((), ())),
            preferred_element_type=F32,
        )
        / TOKENS
    )

    mine = pick(partial, x, 0)
    got = [swap(pick(partial, x ^ k, 0).astype(BF), "x", k) for k in (1, 3, 2)]
    for block in got:
        mine = mine + block.astype(F32)
    mine = after(mine, gate_factor)
    result = pick(mine, zl >> 1, 0)
    for k in (1, 2, 3):
        send = pick(mine, (zl ^ k) >> 1, 0).astype(BF)
        result = result + lax.ppermute(send, ("core", "zl"), home_pairs(k)).astype(F32)
    result = result.astype(BF)
    other_half = swap(result[1], "core", 1)
    input_grad = jnp.where((zl & 1) == core, result[0], other_half)
    return (input_grad, gate_factor)


def solution(mesh):
    fine = Mesh(mesh.devices.reshape(SIZES), AXES)
    return jax.shard_map(
        shards,
        mesh=fine,
        in_specs=(P(COL, ROW), P(ROW, COL), P(ROW, COL), P(ROW, COL), P(ROW, COL), P(COL, ROW)),
        out_specs=(P(COL, ROW), P(ROW, COL)),
        check_vma=False,
    )
```

```python
import jax
import jax.numpy as jnp
from jax import lax
from jax.sharding import Mesh
from jax.sharding import PartitionSpec as P

TOKENS = 1024
ROWS = 32
BF = jnp.bfloat16
F32 = jnp.float32
SIZES = (2, 4, 2, 4, 4)
AXES = ("zh", "y", "core", "x", "zl")
ROW = ("zh", "y", "core")
COL = ("x", "zl")


def swap(block, axis, k):
    n = SIZES[AXES.index(axis)]
    return lax.ppermute(block, axis, [(i, i ^ k) for i in range(n)])


def after(block, *deps):
    return lax.optimization_barrier((block, deps))[0]


def put(buf, block, index, axis):
    start = [0] * buf.ndim
    start[axis] = index
    return lax.dynamic_update_slice(buf, jnp.expand_dims(block, axis), start)


def pick(array, index, axis):
    return lax.dynamic_index_in_dim(array, index, axis, keepdims=False)


def swiglu_grads(hidden_grad, gate_preact, up_preact):
    gate_float = gate_preact.astype(F32)
    up_float = up_preact.astype(F32)
    logistic = jax.nn.sigmoid(gate_float)
    derivative = logistic * (1.0 + gate_float * (1.0 - logistic))
    grad_gate = (hidden_grad * up_float * derivative).astype(BF)
    grad_up = (hidden_grad * gate_float * logistic).astype(BF)
    return (grad_gate, grad_up)


def contract_last(left, right):
    return lax.dot_general(left, right, (((1,), (1,)), ((), ())), preferred_element_type=F32)


def device(zh, y, core, x, zl):
    return (((zh * 4 + y) * 2 + core) * 4 + x) * 4 + zl


def scatter_pairs(half):
    return [
        (
            device(zh, y, core, zh, zl),
            device(zh, zl, half, (core ^ half) * 2 + (y >> 1), 1 + (y & 1)),
        )
        for zh in range(2)
        for y in range(4)
        for core in range(2)
        for zl in range(4)
    ]


def shards(output_grad, gate_preact, up_preact, gate_weight, up_weight, down_weight):
    zh, y, core, x, zl = (lax.axis_index(a) for a in AXES)
    units = gate_preact.shape[1]
    half_units = units // 2
    width = output_grad.shape[1]

    def at_zl(buf, block, which):
        start = ((which & 1) ^ core, which >> 1, 0, 0)
        return lax.dynamic_update_slice(buf, block[None, None], start)

    down_far = swap(down_weight, "core", 1)
    run = at_zl(jnp.zeros((2, 2, 64, width), BF), output_grad, zl)
    for k in (1, 2, 3):
        run = at_zl(run, swap(output_grad, "zl", k), zl ^ k)
    pre_a = jnp.stack([gate_preact[:ROWS], up_preact[:ROWS]])
    pre_b = jnp.stack([gate_preact[ROWS:], up_preact[ROWS:]])
    weights = jnp.concatenate([gate_weight, up_weight], 1)
    run, pre_a = after((run, pre_a), down_far)
    pre_far_a = swap(pre_a, "zh", 1)
    cot = put(jnp.zeros((2, 4, 2, 64, width), BF), run, x, 1)
    for k in (1, 3, 2):
        cot = put(cot, swap(run, "x", k), x ^ k, 1)
    far = swap(cot[1], "core", 1)
    near, far, pre_b = after((cot[0], far, pre_b), pre_far_a)
    pre_far_b = swap(pre_b, "zh", 1)

    def part_of(c):
        rows = slice(c * ROWS, (c + 1) * ROWS)
        part = contract_last(near[:, :, rows].reshape(8 * ROWS, width), down_weight)
        part = part + contract_last(far[:, :, rows].reshape(8 * ROWS, width), down_far)
        return part.reshape(2, 4, ROWS, units)

    def over_y(part, *deps):
        sends = tuple(pick(part, y ^ k, 1).astype(BF) for k in (1, 3, 2))
        sends = after(sends, *deps)
        return [swap(s, "y", k) for s, k in zip(sends, (1, 3, 2))]

    def add_up(part, got):
        hidden = pick(part, y, 1)
        for block in got:
            hidden = hidden + block.astype(F32)
        return hidden

    def grads(hidden, far_hidden, pre, pre_far):
        hidden = hidden + far_hidden.astype(F32)
        low = jnp.where(zh == 0, pre, pre_far)
        high = jnp.where(zh == 0, pre_far, pre)
        gate_tok = jnp.stack([low[0], high[0]])
        up_tok = jnp.stack([low[1], high[1]])
        return jnp.concatenate(swiglu_grads(hidden, gate_tok, up_tok), 2)

    part_a = part_of(0)
    part_b = part_of(1)
    got_a = over_y(part_a)
    hidden_a = add_up(part_a, got_a)
    got_b = over_y(part_b, *got_a, pre_far_b)
    hfar_a = swap(hidden_a.astype(BF), "zh", 1)
    both_a = grads(hidden_a, hfar_a, pre_a, pre_far_a)
    hidden_b = add_up(part_b, got_b)
    hfar_b = swap(hidden_b.astype(BF), "zh", 1)
    both_b = grads(hidden_b, hfar_b, pre_b, pre_far_b)
    both = jnp.concatenate([both_a, both_b], 1)

    pieces = [
        lax.ppermute(
            both[:, :, half * half_units : (half + 1) * half_units], AXES, scatter_pairs(half)
        )
        for half in range(2)
    ]
    one = swap(both, "y", 1)
    three = swap(both, "y", 3)
    one, three, *pieces = lax.optimization_barrier((one, three, *pieces))
    two0 = swap(one[0], "y", 3)
    two1 = swap(three[1], "y", 1)
    piece = jnp.where(core == 0, pieces[0], pieces[1])
    edge = lax.ppermute(piece, "zl", [(1, 0), (2, 3)])
    mid = lax.ppermute(piece, "zl", [(1, 2), (2, 1)])
    cross = lax.ppermute(piece, "zl", [(1, 3), (2, 0)])
    srun = jnp.stack(
        [lax.select_n(zl, edge, piece, mid, cross), lax.select_n(zl, cross, mid, piece, edge)]
    )
    two0, two1, srun = lax.optimization_barrier((two0, two1, srun))
    got = [swap(srun, "x", k) for k in (1, 3, 2)]
    ring = jnp.stack([one, three])
    two = jnp.stack([two0, two1])
    both_other = swap(both, "core", 1)
    ring_other = swap(ring, "core", 1)
    two_other = swap(two, "core", 1)

    def assemble(both, ring, two):
        full = jnp.zeros((4, 2, 64, 2 * units), BF)
        for block, k in ((both, 0), (ring[0], 1), (ring[1], 3), (two, 2)):
            full = put(full, block, y ^ k, 0)
        return full

    full = assemble(both, ring, two)
    full_other = assemble(both_other, ring_other, two_other)

    partial = jnp.stack(
        [contract_last(f.reshape(512, 2 * units), weights) for f in (full, full_other)]
    )
    partial = partial.reshape(2, 2, 2, 2, 64, width).transpose(3, 1, 2, 0, 4, 5)
    partial = partial.reshape(4, 4, 64, width)

    slab = put(jnp.zeros((4, 2, 2, 64, half_units), BF), srun, x, 0)
    for block, k in zip(got, (1, 3, 2)):
        slab = put(slab, block, x ^ k, 0)
    gate_all = jnp.stack([full[..., :units], full_other[..., :units]])
    gate_factor = (
        lax.dot_general(
            slab.reshape(TOKENS, half_units),
            gate_all.reshape(TOKENS, units),
            (((0,), (0,)), ((), ())),
            preferred_element_type=F32,
        )
        / TOKENS
    )

    mine = pick(partial, x, 0)
    got = [swap(pick(partial, x ^ k, 0).astype(BF), "x", k) for k in (1, 3, 2)]
    for block in got:
        mine = mine + block.astype(F32)
    mine = after(mine, gate_factor)

    def for_zl(column):
        return pick(mine, (column >> 1) * 2 + ((column & 1) ^ core), 0)

    result = for_zl(zl)
    for k in (1, 2, 3):
        result = result + swap(for_zl(zl ^ k).astype(BF), "zl", k).astype(F32)
    return (result.astype(BF), gate_factor)


def solution(mesh):
    fine = Mesh(mesh.devices.reshape(SIZES), AXES)
    return jax.shard_map(
        shards,
        mesh=fine,
        in_specs=(P(COL, ROW), P(ROW, COL), P(ROW, COL), P(ROW, COL), P(ROW, COL), P(COL, ROW)),
        out_specs=(P(COL, ROW), P(ROW, COL)),
        check_vma=False,
    )
```

```python
import jax
import jax.numpy as jnp
from jax import lax
from jax.sharding import Mesh
from jax.sharding import PartitionSpec as P

TOKENS = 1024
ROWS = 32
BF = jnp.bfloat16
F32 = jnp.float32
SIZES = (2, 4, 2, 4, 4)
AXES = ("zh", "y", "core", "x", "zl")
ROW = ("zh", "y", "core")
COL = ("x", "zl")


def swap(block, axis, k):
    n = SIZES[AXES.index(axis)]
    return lax.ppermute(block, axis, [(i, i ^ k) for i in range(n)])


def after(block, *deps):
    return lax.optimization_barrier((block, deps))[0]


def put(buf, block, index, axis):
    start = [0] * buf.ndim
    start[axis] = index
    return lax.dynamic_update_slice(buf, jnp.expand_dims(block, axis), start)


def pick(array, index, axis):
    return lax.dynamic_index_in_dim(array, index, axis, keepdims=False)


def swiglu_grads(hidden_grad, gate_preact, up_preact):
    gate_float = gate_preact.astype(F32)
    up_float = up_preact.astype(F32)
    logistic = jax.nn.sigmoid(gate_float)
    derivative = logistic * (1.0 + gate_float * (1.0 - logistic))
    grad_gate = (hidden_grad * up_float * derivative).astype(BF)
    grad_up = (hidden_grad * gate_float * logistic).astype(BF)
    return (grad_gate, grad_up)


def contract_last(left, right):
    return lax.dot_general(left, right, (((1,), (1,)), ((), ())), preferred_element_type=F32)


def device(zh, y, core, x, zl):
    return (((zh * 4 + y) * 2 + core) * 4 + x) * 4 + zl


def scatter_pairs(half):
    return [
        (
            device(zh, y, core, zh, zl),
            device(zh, zl, half, (core ^ half) * 2 + (y >> 1), 1 + ((y ^ zl) & 1)),
        )
        for zh in range(2)
        for y in range(4)
        for core in range(2)
        for zl in range(4)
    ]


def shards(output_grad, gate_preact, up_preact, gate_weight, up_weight, down_weight):
    zh, y, core, x, zl = (lax.axis_index(a) for a in AXES)
    units = gate_preact.shape[1]
    half_units = units // 2
    width = output_grad.shape[1]

    def at_zl(buf, block, which):
        start = ((which & 1) ^ core, which >> 1, 0, 0)
        return lax.dynamic_update_slice(buf, block[None, None], start)

    down_far = swap(down_weight, "core", 1)
    run = at_zl(jnp.zeros((2, 2, 64, width), BF), output_grad, zl)
    for k in (1, 2, 3):
        run = at_zl(run, swap(output_grad, "zl", k), zl ^ k)
    pre_a = jnp.stack([gate_preact[:ROWS], up_preact[:ROWS]])
    pre_b = jnp.stack([gate_preact[ROWS:], up_preact[ROWS:]])
    weights = jnp.concatenate([gate_weight, up_weight], 1)
    run, pre_a = after((run, pre_a), down_far)
    pre_far_a = swap(pre_a, "zh", 1)
    cot = put(jnp.zeros((2, 4, 2, 64, width), BF), run, x, 1)
    for k in (1, 3, 2):
        cot = put(cot, swap(run, "x", k), x ^ k, 1)
    far = swap(cot[1], "core", 1)
    near, far, pre_b = after((cot[0], far, pre_b), pre_far_a)
    pre_far_b = swap(pre_b, "zh", 1)

    def part_of(c):
        rows = slice(c * ROWS, (c + 1) * ROWS)
        part = contract_last(near[:, :, rows].reshape(8 * ROWS, width), down_weight)
        part = part + contract_last(far[:, :, rows].reshape(8 * ROWS, width), down_far)
        return part.reshape(2, 4, ROWS, units)

    def over_y(part, *deps):
        sends = tuple(pick(part, y ^ k, 1).astype(BF) for k in (1, 3, 2))
        sends = after(sends, *deps)
        return [swap(s, "y", k) for s, k in zip(sends, (1, 3, 2))]

    def add_up(part, got):
        hidden = pick(part, y, 1)
        for block in got:
            hidden = hidden + block.astype(F32)
        return hidden

    def grads(hidden, far_hidden, pre, pre_far):
        hidden = hidden + far_hidden.astype(F32)
        low = jnp.where(zh == 0, pre, pre_far)
        high = jnp.where(zh == 0, pre_far, pre)
        gate_tok = jnp.stack([low[0], high[0]])
        up_tok = jnp.stack([low[1], high[1]])
        return jnp.concatenate(swiglu_grads(hidden, gate_tok, up_tok), 2)

    part_a = part_of(0)
    part_b = part_of(1)
    got_a = over_y(part_a)
    hidden_a = add_up(part_a, got_a)
    got_b = over_y(part_b, *got_a)
    hfar_a = swap(hidden_a.astype(BF), "zh", 1)
    both_a = grads(hidden_a, hfar_a, pre_a, pre_far_a)
    hidden_b = add_up(part_b, got_b)
    hfar_b = swap(hidden_b.astype(BF), "zh", 1)
    both_b = grads(hidden_b, hfar_b, pre_b, pre_far_b)
    both = jnp.concatenate([both_a, both_b], 1)

    pieces = [
        lax.ppermute(
            both[:, :, half * half_units : (half + 1) * half_units], AXES, scatter_pairs(half)
        )
        for half in range(2)
    ]
    one = swap(both, "y", 1)
    three = swap(both, "y", 3)
    one, three, *pieces = lax.optimization_barrier((one, three, *pieces))
    two0 = swap(one[0], "y", 3)
    two1 = swap(three[1], "y", 1)
    piece = jnp.where(core == 0, pieces[0], pieces[1])
    edge = lax.ppermute(piece, "zl", [(1, 0), (2, 3)])
    mid = lax.ppermute(piece, "zl", [(1, 2), (2, 1)])
    cross = lax.ppermute(piece, "zl", [(1, 3), (2, 0)])
    first = lax.select_n(zl, edge, piece, mid, cross)
    second = lax.select_n(zl, cross, mid, piece, edge)
    even = (y & 1) == 0
    srun = jnp.stack([jnp.where(even, first, second), jnp.where(even, second, first)])

    def fill(full, blocks):
        for block, k in blocks:
            full = put(full, block, y ^ k, 0)
        return full

    ring = jnp.stack([both, one, three])
    ring_other = swap(ring, "core", 1)
    empty = jnp.zeros((4, 2, 64, 2 * units), BF)
    full = fill(empty, ((both, 0), (one, 1), (three, 3)))
    two0, two1, srun, full = lax.optimization_barrier((two0, two1, srun, full))
    near_1 = swap(srun, "x", 1)
    near_3 = swap(srun, "x", 3)
    two = jnp.stack([two0, two1])
    full = fill(full, ((two, 2),))
    two_other = swap(two, "core", 1)
    full_other = fill(
        empty, ((ring_other[0], 0), (ring_other[1], 1), (ring_other[2], 3), (two_other, 2))
    )

    partial = jnp.stack(
        [contract_last(f.reshape(512, 2 * units), weights) for f in (full, full_other)]
    )
    partial = partial.reshape(2, 2, 2, 2, 64, width).transpose(3, 1, 2, 0, 4, 5)
    partial = partial.reshape(4, 4, 64, width)

    near_1, near_3, partial = lax.optimization_barrier((near_1, near_3, partial))
    across = jnp.stack([swap(near_1[0], "x", 3), swap(near_3[1], "x", 1)])
    slab = put(jnp.zeros((4, 2, 2, 64, half_units), BF), srun, x, 0)
    for block, k in ((near_1, 1), (near_3, 3), (across, 2)):
        slab = put(slab, block, x ^ k, 0)
    gate_all = jnp.stack([full[..., :units], full_other[..., :units]])
    gate_factor = (
        lax.dot_general(
            slab.reshape(TOKENS, half_units),
            gate_all.reshape(TOKENS, units),
            (((0,), (0,)), ((), ())),
            preferred_element_type=F32,
        )
        / TOKENS
    )

    mine = pick(partial, x, 0)
    got = [swap(pick(partial, x ^ k, 0).astype(BF), "x", k) for k in (1, 3, 2)]
    for block in got:
        mine = mine + block.astype(F32)

    def for_zl(column):
        return pick(mine, (column >> 1) * 2 + ((column & 1) ^ core), 0)

    result = for_zl(zl)
    for k in (1, 2, 3):
        result = result + swap(for_zl(zl ^ k).astype(BF), "zl", k).astype(F32)
    return (result.astype(BF), gate_factor)


def solution(mesh):
    fine = Mesh(mesh.devices.reshape(SIZES), AXES)
    return jax.shard_map(
        shards,
        mesh=fine,
        in_specs=(P(COL, ROW), P(ROW, COL), P(ROW, COL), P(ROW, COL), P(ROW, COL), P(COL, ROW)),
        out_specs=(P(COL, ROW), P(ROW, COL)),
        check_vma=False,
    )
```

```python
import jax
import jax.numpy as jnp
from jax import lax
from jax.sharding import Mesh
from jax.sharding import PartitionSpec as P

TOKENS = 1024
ROWS = 32
BF = jnp.bfloat16
F32 = jnp.float32
SIZES = (2, 4, 2, 4, 4)
AXES = ("zh", "y", "core", "x", "zl")
ROW = ("zh", "y", "core")
COL = ("x", "zl")


def swap(block, axis, k):
    n = SIZES[AXES.index(axis)]
    return lax.ppermute(block, axis, [(i, i ^ k) for i in range(n)])


def after(block, *deps):
    return lax.optimization_barrier((block, deps))[0]


def put(buf, block, index, axis):
    start = [0] * buf.ndim
    start[axis] = index
    return lax.dynamic_update_slice(buf, jnp.expand_dims(block, axis), start)


def pick(array, index, axis):
    return lax.dynamic_index_in_dim(array, index, axis, keepdims=False)


def swiglu_grads(hidden_grad, gate_preact, up_preact):
    gate_float = gate_preact.astype(F32)
    up_float = up_preact.astype(F32)
    logistic = jax.nn.sigmoid(gate_float)
    derivative = logistic * (1.0 + gate_float * (1.0 - logistic))
    grad_gate = (hidden_grad * up_float * derivative).astype(BF)
    grad_up = (hidden_grad * gate_float * logistic).astype(BF)
    return (grad_gate, grad_up)


def contract_last(left, right):
    return lax.dot_general(left, right, (((1,), (1,)), ((), ())), preferred_element_type=F32)


def device(zh, y, core, x, zl):
    return (((zh * 4 + y) * 2 + core) * 4 + x) * 4 + zl


def scatter_pairs(half):
    return [
        (
            device(zh, y, core, zh, zl),
            device(zh, zl, half, (core ^ half) * 2 + (y >> 1), 1 + ((y ^ zl) & 1)),
        )
        for zh in range(2)
        for y in range(4)
        for core in range(2)
        for zl in range(4)
    ]


def shards(output_grad, gate_preact, up_preact, gate_weight, up_weight, down_weight):
    zh, y, core, x, zl = (lax.axis_index(a) for a in AXES)
    units = gate_preact.shape[1]
    half_units = units // 2
    width = output_grad.shape[1]

    def at_zl(buf, block, which):
        start = ((which & 1) ^ core, which >> 1, 0, 0)
        return lax.dynamic_update_slice(buf, block[None, None], start)

    down_far = swap(down_weight, "core", 1)
    run = at_zl(jnp.zeros((2, 2, 64, width), BF), output_grad, zl)
    for k in (1, 2, 3):
        run = at_zl(run, swap(output_grad, "zl", k), zl ^ k)
    pre_a = jnp.stack([gate_preact[:ROWS], up_preact[:ROWS]])
    pre_b = jnp.stack([gate_preact[ROWS:], up_preact[ROWS:]])
    weights = jnp.concatenate([gate_weight, up_weight], 1)
    run, pre_a = after((run, pre_a), down_far)
    pre_far_a = swap(pre_a, "zh", 1)
    cot = put(jnp.zeros((2, 4, 2, 64, width), BF), run, x, 1)
    for k in (1, 3, 2):
        cot = put(cot, swap(run, "x", k), x ^ k, 1)
    far = swap(cot[1], "core", 1)
    near, far, pre_b = after((cot[0], far, pre_b), pre_far_a)
    pre_far_b = swap(pre_b, "zh", 1)

    def part_of(c):
        rows = slice(c * ROWS, (c + 1) * ROWS)
        part = contract_last(near[:, :, rows].reshape(8 * ROWS, width), down_weight)
        part = part + contract_last(far[:, :, rows].reshape(8 * ROWS, width), down_far)
        return part.reshape(2, 4, ROWS, units)

    def over_y(part, *deps):
        sends = tuple(pick(part, y ^ k, 1).astype(BF) for k in (1, 3, 2))
        sends = after(sends, *deps)
        return [swap(s, "y", k) for s, k in zip(sends, (1, 3, 2))]

    def add_up(part, got):
        hidden = pick(part, y, 1)
        for block in got:
            hidden = hidden + block.astype(F32)
        return hidden

    def grads(hidden, far_hidden, pre, pre_far):
        hidden = hidden + far_hidden.astype(F32)
        low = jnp.where(zh == 0, pre, pre_far)
        high = jnp.where(zh == 0, pre_far, pre)
        gate_tok = jnp.stack([low[0], high[0]])
        up_tok = jnp.stack([low[1], high[1]])
        return jnp.concatenate(swiglu_grads(hidden, gate_tok, up_tok), 2)

    part_a = part_of(0)
    part_b = part_of(1)
    got_a = over_y(part_a)
    hidden_a = add_up(part_a, got_a)
    got_b = over_y(part_b, *got_a)
    hfar_a = swap(hidden_a.astype(BF), "zh", 1)
    both_a = grads(hidden_a, hfar_a, pre_a, pre_far_a)
    hidden_b = add_up(part_b, got_b)
    hfar_b = swap(hidden_b.astype(BF), "zh", 1)
    both_b = grads(hidden_b, hfar_b, pre_b, pre_far_b)
    both = jnp.concatenate([both_a, both_b], 1)

    pieces = [
        lax.ppermute(
            both[:, :, half * half_units : (half + 1) * half_units], AXES, scatter_pairs(half)
        )
        for half in range(2)
    ]
    one = swap(both, "y", 1)
    three = swap(both, "y", 3)
    one, three, *pieces = lax.optimization_barrier((one, three, *pieces))
    two0 = swap(one[0], "y", 3)
    two1 = swap(three[1], "y", 1)
    piece = jnp.where(core == 0, pieces[0], pieces[1])
    edge = lax.ppermute(piece, "zl", [(1, 0), (2, 3)])
    mid = lax.ppermute(piece, "zl", [(1, 2), (2, 1)])
    cross = lax.ppermute(piece, "zl", [(1, 3), (2, 0)])
    first = lax.select_n(zl, edge, piece, mid, cross)
    second = lax.select_n(zl, cross, mid, piece, edge)
    even = (y & 1) == 0
    srun = jnp.stack([jnp.where(even, first, second), jnp.where(even, second, first)])

    def fill(full, blocks):
        for block, k in blocks:
            full = put(full, block, y ^ k, 0)
        return full

    ring = jnp.stack([both, one, three])
    ring_other = swap(ring, "core", 1)
    empty = jnp.zeros((4, 2, 64, 2 * units), BF)
    full = fill(empty, ((both, 0), (one, 1), (three, 3)))
    two0, two1, srun, full = lax.optimization_barrier((two0, two1, srun, full))
    near_1 = swap(srun, "x", 1)
    near_3 = swap(srun, "x", 3)
    two = jnp.stack([two0, two1])
    full = fill(full, ((two, 2),))
    two_other = swap(two, "core", 1)
    full_other = fill(
        empty, ((ring_other[0], 0), (ring_other[1], 1), (ring_other[2], 3), (two_other, 2))
    )

    partial = jnp.stack(
        [contract_last(f.reshape(512, 2 * units), weights) for f in (full, full_other)]
    )
    partial = partial.reshape(2, 2, 2, 2, 64, width).transpose(3, 1, 2, 0, 4, 5)
    partial = partial.reshape(4, 4, 64, width)

    near_1, near_3, partial = lax.optimization_barrier((near_1, near_3, partial))
    across = jnp.stack([swap(near_1[0], "x", 3), swap(near_3[1], "x", 1)])
    slab = put(jnp.zeros((4, 2, 2, 64, half_units), BF), srun, x, 0)
    for block, k in ((near_1, 1), (near_3, 3)):
        slab = put(slab, block, x ^ k, 0)
    gate_all = jnp.stack([full[..., :units], full_other[..., :units]])
    gate_last = pick(gate_all.reshape(4, 256, units), x ^ 2, 0)

    def contract_first(left, right):
        return lax.dot_general(left, right, (((0,), (0,)), ((), ())), preferred_element_type=F32)

    early = contract_first(slab.reshape(TOKENS, half_units), gate_all.reshape(TOKENS, units))
    late = contract_first(across.reshape(256, half_units), gate_last)
    gate_factor = (early + late) / TOKENS

    mine = pick(partial, x, 0)
    got = [swap(pick(partial, x ^ k, 0).astype(BF), "x", k) for k in (1, 3, 2)]
    for block in got:
        mine = mine + block.astype(F32)

    def for_zl(column):
        return pick(mine, (column >> 1) * 2 + ((column & 1) ^ core), 0)

    result = for_zl(zl)
    for k in (1, 2, 3):
        result = result + swap(for_zl(zl ^ k).astype(BF), "zl", k).astype(F32)
    return (result.astype(BF), gate_factor)


def solution(mesh):
    fine = Mesh(mesh.devices.reshape(SIZES), AXES)
    return jax.shard_map(
        shards,
        mesh=fine,
        in_specs=(P(COL, ROW), P(ROW, COL), P(ROW, COL), P(ROW, COL), P(ROW, COL), P(COL, ROW)),
        out_specs=(P(COL, ROW), P(ROW, COL)),
        check_vma=False,
    )
```
